32 devices in a mesh: dp: 8 (over y, x, core), expert: 4 (over z).
Axes of the slice: x: 2, y: 2, z: 4, core: 2. Of those that a mesh axis runs over, the one named last changes fastest.
Arguments:
- tokens: bfloat16 [2048, 4096], P('dp', 'expert'), may hold values from -100 to 100
- w_gate: bfloat16 [4, 4096, 14336], P('expert', None, 'dp'), may hold values from -0.09375 to 0.09375
- w_up: bfloat16 [4, 4096, 14336], P('expert', None, 'dp'), may hold values from -0.09375 to 0.09375
- w_down: bfloat16 [4, 14336, 4096], P('expert', 'dp'), may hold values from -0.046875 to 0.046875
- pick_block: int32 [4, 4], replicated, may hold values from 0 to 3
- pick_live: int32 [4, 4], replicated, may hold values from 0 to 1, as said below
- combine_weight: float32 [4, 4], replicated, may hold values from 0.25 to 1
Outputs:
- combined: bfloat16 [2048, 4096], P('dp', 'expert')
The draws below stay inside these ranges and needn't reach their ends.
Inputs may be any that keep to these rules, and one draw needn't show every extreme that they name: `pick_live`: each expert takes at least one block, and some expert takes a block from every pair of dp rows.
All inputs are finite; a program needn't handle non-finite values.
Results may differ from the reference program's by a relative error of at most 0.02.
Values may be sent and summed in bfloat16 or wider, within the bound.
No kernel may reach another device: no remote copies, remote signals or barrier semaphores. Data moves between devices by JAX's collectives and lax.ppermute only.
A program may use at most 128 MiB of HBM per device.

```python
import math
import jax
import jax.numpy as jnp
from jax import lax

D = 4096
FF = 14336
BLOCK = 128
BLK_ROW = 2
EXPERTS = 4
PAIRS = 4
HID_DEV = 1792
TOKENS = 2048
N_DP = 8


def draw_tokens(key, part):
    key_base, key_row, key_col = jax.random.split(key, 3)
    col_scale = jnp.exp(jax.random.uniform(key_col, (1, D), jnp.float32, math.log(0.5), math.log(2.0)))
    base_values = jax.random.normal(key_base, (TOKENS, D), jnp.float32)
    row_scale = jnp.exp(jax.random.uniform(key_row, (TOKENS, 1), jnp.float32, math.log(0.3), math.log(3.0)))
    values = jnp.clip(base_values * row_scale * col_scale, -100.0, 100.0)
    return values.astype(jnp.bfloat16)


def draw_pick_live(key, part):
    key_count, key_full, key_order = jax.random.split(key, 3)
    counts = jax.random.randint(key_count, (EXPERTS,), 1, PAIRS + 1)
    full_one = jax.random.randint(key_full, (), 0, EXPERTS)
    counts = jnp.where(jnp.arange(EXPERTS) == full_one, PAIRS, counts)
    ranking = jax.vmap(lambda sub_key: jax.random.permutation(sub_key, PAIRS))(jax.random.split(key_order, EXPERTS))
    return (ranking < counts[:, None]).astype(jnp.int32)


def set_ends(array, own_key, smallest, top_value):
    index_at = [jax.random.randint(jax.random.fold_in(own_key, axis), (), 0, length) for axis, length in enumerate(array.shape)]
    longest = array.shape.index(max(array.shape))
    beside = index_at[:longest] + [(index_at[longest] + 1) % array.shape[longest]] + index_at[longest + 1:]
    return array.at[tuple(index_at)].set(smallest).at[tuple(beside)].set(top_value)


def level_of(stream_key, dims, shards, smallest, high):
    def one(position, shards_of):
        steps = jax.random.uniform(jax.random.fold_in(jax.random.fold_in(stream_key, 6), position), (shards_of,), jnp.float32, smallest / len(shards), high / len(shards))
        return jnp.repeat(jnp.exp(steps), dims[position] // shards_of).reshape((-1,) + (1,) * (len(dims) - position - 1))

    level = one(*shards[0])
    for cut in shards[1:]:
        level = level * one(*cut)
    return level


def scatter_about(rng, shape, scale, most, cuts=(), kind=jnp.bfloat16):
    entries = jax.random.normal(rng, shape, jnp.float32) * scale
    if len(cuts) > 0:
        entries = level_of(rng, shape, cuts, -0.22, 0.18) * entries
    return jnp.clip(entries, min=-most, max=most).astype(kind)


def setup_inputs(seed: int = 0) -> dict:
    seeds = jax.random.split(jax.random.key(seed), 8)
    return {
        "tokens": draw_tokens(jax.random.fold_in(seeds[7], 71), 0),
        "w_gate": scatter_about(seeds[1], (EXPERTS, D, FF), D ** -0.5, 0.09375, ((0, 4), (2, 8))),
        "w_up": scatter_about(seeds[2], (EXPERTS, D, FF), D ** -0.5, 0.09375, ((0, 4), (2, 8))),
        "w_down": scatter_about(seeds[3], (EXPERTS, FF, D), FF ** -0.5, 0.046875, ((0, 4), (1, 8))),
        "pick_block": set_ends(jax.random.randint(seeds[4], (EXPERTS, PAIRS), 0, 2 * BLK_ROW), jax.random.fold_in(seeds[4], 1), 0, (2 * BLK_ROW) - 1).astype(jnp.int32),
        "pick_live": draw_pick_live(jax.random.fold_in(seeds[7], 71), 0),
        "combine_weight": jnp.clip(jnp.exp(jax.random.uniform(seeds[6], (EXPERTS, PAIRS), jnp.float32, math.log(0.25), math.log(1.0))), 0.25, 1.0),
    }


def reference(tokens, w_gate, w_up, w_down, pick_block, pick_live, combine_weight):
    tokens_f32 = tokens.astype(jnp.float32)
    inv_rms = lax.rsqrt(lax.optimization_barrier(jnp.mean(tokens_f32 * tokens_f32, axis=1, keepdims=True)) + 1e-05)
    normed = (tokens_f32 * inv_rms).astype(jnp.bfloat16)
    blocks = normed.reshape(TOKENS // BLOCK, BLOCK, D)
    combined = jnp.zeros((TOKENS // BLOCK, BLOCK, D), jnp.float32)
    pair_ids = jnp.arange(PAIRS, dtype=jnp.int32)
    for expert in range(EXPERTS):
        block_index = (2 * BLK_ROW * pair_ids + pick_block[expert]).astype(jnp.int32)
        live_mask = pick_live[expert] == 1
        chosen = jnp.where(live_mask[:, None, None], blocks[block_index], jnp.zeros((), jnp.bfloat16))
        chosen = chosen.reshape(PAIRS * BLOCK, D)
        gate_proj = jnp.dot(chosen, w_gate[expert], preferred_element_type=jnp.float32)
        up_proj = jnp.dot(chosen, w_up[expert], preferred_element_type=jnp.float32)
        hidden = (jax.nn.silu(gate_proj) * up_proj).astype(jnp.bfloat16)
        summed = jnp.zeros((PAIRS * BLOCK, D), jnp.float32)
        for group_index in range(N_DP):
            lower = group_index * HID_DEV
            partial_value = jnp.dot(hidden[:, lower:lower + HID_DEV], w_down[expert, lower:lower + HID_DEV], preferred_element_type=jnp.float32).astype(jnp.bfloat16)
            summed = summed + lax.optimization_barrier(partial_value).astype(jnp.float32)
        expert_out = lax.optimization_barrier(summed.astype(jnp.bfloat16)).astype(jnp.float32)
        weighting = jnp.where(live_mask, combine_weight[expert], jnp.zeros((), jnp.float32))
        combined = combined.at[block_index].add(weighting[:, None, None] * expert_out.reshape(PAIRS, BLOCK, D))
    return combined.astype(jnp.bfloat16).reshape(TOKENS, D)
```

```python
import functools

import jax
import jax.numpy as jnp
from jax import lax
from jax.experimental import pallas as pl
from jax.experimental.pallas import tpu as pltpu
from jax.sharding import PartitionSpec as P

BLOCK = 128
HALF = BLOCK // 2
VMEM_LIMIT = 40 * 1024 * 1024
GROUPS = ((0,), (1,), (2,), (3,))


def exchange(value, axis, offset):
    count = lax.axis_size(axis)
    return lax.ppermute(value, axis, [(i, i ^ offset) for i in range(count)])


def col_block(width, most):
    best = 128
    for size in range(128, most + 1, 128):
        if width % size == 0:
            best = size
    return best


def top_bit(value):
    return 1 << (value.bit_length() - 1)


def low_bit(value):
    return value & -value


def gather_pieces(own, chips):
    rows = own.shape[0] // 2
    got = {0: own}
    for j in range(1, chips):
        if top_bit(j) == j:
            got[j] = exchange(own, "dp", 2 * j)
    for j in range(1, chips):
        if top_bit(j) != j:
            top, low = top_bit(j), low_bit(j)
            first = exchange(got[j ^ top][:rows], "dp", 2 * top)
            second = exchange(got[j ^ low][rows:], "dp", 2 * low)
            got[j] = jnp.concatenate([first, second], axis=0)
    return jnp.concatenate([got[j] for j in range(chips)], axis=0)


def add_rounded(a, b):
    return (a.astype(jnp.float32) + b.astype(jnp.float32)).astype(jnp.bfloat16)


def scatter_pieces(sums, chips):
    rows = sums[0].shape[0] // 2
    halves = {j: [sums[j][:rows], sums[j][rows:]] for j in range(chips)}
    for j in range(chips - 1, 0, -1):
        if top_bit(j) != j:
            top, low = top_bit(j), low_bit(j)
            first = exchange(halves[j][0], "dp", 2 * top)
            second = exchange(halves[j][1], "dp", 2 * low)
            halves[j ^ top][0] = add_rounded(halves[j ^ top][0], first)
            halves[j ^ low][1] = add_rounded(halves[j ^ low][1], second)
    total = sums[0].astype(jnp.float32)
    for j in range(1, chips):
        if top_bit(j) == j:
            moved = exchange(jnp.concatenate(halves[j], axis=0), "dp", 2 * j)
            total = total + moved.astype(jnp.float32)
    return total.astype(jnp.bfloat16)


def gate_up_kernel(count, first, last, model_width, ids, *refs):
    x_refs = refs[: 2 * count]
    wg_refs = refs[2 * count : 3 * count]
    wu_refs = refs[3 * count : 4 * count]
    refs = refs[4 * count :]
    if not first:
        gate_in, up_in, squares_in = refs[:3]
        refs = refs[3:]
    if last:
        hidden_out, xs, squares = refs
    else:
        gate_out, up_out, squares_out, xs = refs
        squares = squares_out
    features = x_refs[0].shape[1]
    half = x_refs[0].shape[0]

    @pl.when(pl.program_id(0) == 0)
    def _():
        for c in range(count):
            for k in range(2):
                xs[k * half : (k + 1) * half, c * features : (c + 1) * features] = x_refs[2 * c + k][...]
        total = jnp.zeros((2 * half, 1), jnp.float32)
        for c in range(count):
            values = xs[:, c * features : (c + 1) * features].astype(jnp.float32)
            total = total + jnp.sum(values * values, axis=1, keepdims=True)
        total = jnp.broadcast_to(total, squares.shape)
        if not first:
            total = total + squares_in[...]
        squares[...] = total

    gate = None if first else gate_in[...]
    up = None if first else up_in[...]
    for c in range(count):
        part = xs[:, c * features : (c + 1) * features]
        dot_gate = jnp.dot(part, wg_refs[c][0], preferred_element_type=jnp.float32)
        dot_up = jnp.dot(part, wu_refs[c][0], preferred_element_type=jnp.float32)
        gate = dot_gate if gate is None else gate + dot_gate
        up = dot_up if up is None else up + dot_up
    if last:
        inv_rms = lax.rsqrt(squares[:, :1] / model_width + 1e-05)
        gate = gate * inv_rms
        hidden_out[...] = (gate / (1.0 + jnp.exp(-gate)) * (up * inv_rms)).astype(jnp.bfloat16)
    else:
        gate_out[...] = gate
        up_out[...] = up


def gate_up(ids, pieces, w_gate, w_up, carry, last, model_width):
    count = len(pieces)
    first = carry is None
    half, features = pieces[0][0].shape
    rows = 2 * half
    hid = w_gate.shape[2]
    block = col_block(hid, 256)
    whole = pl.BlockSpec((half, features), lambda j, s: (0, 0))
    weight = [
        pl.BlockSpec((1, features, block), functools.partial(lambda c, j, s: (0, s[c], j), c)) for c in range(count)
    ]
    acc = pl.BlockSpec((rows, block), lambda j, s: (0, j))
    sq = pl.BlockSpec((rows, 128), lambda j, s: (0, 0))
    acc_shape = jax.ShapeDtypeStruct((rows, hid), jnp.float32)
    sq_shape = jax.ShapeDtypeStruct((rows, 128), jnp.float32)
    in_specs = [whole] * (2 * count) + weight + weight + ([] if first else [acc, acc, sq])
    scratch = [pltpu.VMEM((rows, count * features), jnp.bfloat16)]
    if last:
        out_specs, out_shape = acc, jax.ShapeDtypeStruct((rows, hid), jnp.bfloat16)
        scratch.append(pltpu.VMEM((rows, 128), jnp.float32))
    else:
        out_specs, out_shape = [acc, acc, sq], [acc_shape, acc_shape, sq_shape]
    flat = [half_piece for piece in pieces for half_piece in piece]
    return pl.pallas_call(
        functools.partial(gate_up_kernel, count, first, last, model_width),
        grid_spec=pltpu.PrefetchScalarGridSpec(
            num_scalar_prefetch=1,
            grid=(hid // block,),
            in_specs=in_specs,
            out_specs=out_specs,
            scratch_shapes=scratch,
        ),
        out_shape=out_shape,
        cost_estimate=pl.CostEstimate(
            flops=4 * rows * features * count * hid,
            bytes_accessed=4 * features * count * hid,
            transcendentals=0,
        ),
        compiler_params=pltpu.CompilerParams(vmem_limit_bytes=VMEM_LIMIT),
    )(ids, *flat, *[w_gate] * count, *[w_up] * count, *(() if first else carry))


def down_kernel(ids, hidden, weight, mine, other):
    half = mine.shape[0]
    value = jnp.dot(hidden[...], weight[0], preferred_element_type=jnp.float32).astype(jnp.bfloat16)
    mine[...] = value[:half]
    other[...] = value[half:]


def down(ids, hidden, w_down, features):
    rows, hid = hidden.shape
    block = col_block(features, 256)
    steps = features // block
    out = pl.BlockSpec((rows // 2, block), lambda j, s: (0, j))
    shape = jax.ShapeDtypeStruct((rows // 2, features), jnp.bfloat16)
    return pl.pallas_call(
        down_kernel,
        grid_spec=pltpu.PrefetchScalarGridSpec(
            num_scalar_prefetch=1,
            grid=(steps,),
            in_specs=[
                pl.BlockSpec((rows, hid), lambda j, s: (0, 0)),
                pl.BlockSpec((1, hid, block), lambda j, s: (0, 0, s[0] * steps + j)),
            ],
            out_specs=[out, out],
        ),
        out_shape=[shape, shape],
        cost_estimate=pl.CostEstimate(
            flops=2 * rows * hid * features, bytes_accessed=2 * hid * features, transcendentals=0
        ),
        compiler_params=pltpu.CompilerParams(vmem_limit_bytes=VMEM_LIMIT),
    )(ids, hidden, w_down)


def select_kernel(count, sources, live, mine, other, *outs):
    here = mine.shape[0]
    for c in range(count):
        source = sources[c]
        keep = live[c] == 1

        @pl.when(keep & (source < here))
        def _():
            outs[c][...] = mine[jnp.minimum(source, here - 1)]

        @pl.when(keep & (source >= here))
        def _():
            outs[c][...] = other[jnp.maximum(source - here, 0)]

        @pl.when(jnp.logical_not(keep))
        def _():
            outs[c][...] = jnp.zeros_like(outs[c])


def select(sources, live, mine, other, count):
    whole = pl.BlockSpec(memory_space=pltpu.VMEM)
    scalars = pl.BlockSpec(memory_space=pltpu.SMEM)
    shape = jax.ShapeDtypeStruct(mine.shape[1:], jnp.bfloat16)
    return pl.pallas_call(
        functools.partial(select_kernel, count),
        in_specs=[scalars, scalars, whole, whole],
        out_specs=[whole] * count,
        out_shape=[shape] * count,
    )(sources, live, mine, other)


def combine_kernel(count, here, coefs, *refs):
    values = refs[:count]
    mine, other = refs[count:]
    for b in range(2 * here):
        total = None
        for c in range(count):
            term = coefs[c, b] * values[c][...].astype(jnp.float32)
            total = term if total is None else total + term
        target = mine if b < here else other
        target[b % here] = total.astype(jnp.bfloat16)


def combine(coefs, values, here):
    whole = pl.BlockSpec(memory_space=pltpu.VMEM)
    shape = jax.ShapeDtypeStruct((here,) + values[0].shape, jnp.bfloat16)
    return pl.pallas_call(
        functools.partial(combine_kernel, len(values), here),
        in_specs=[pl.BlockSpec(memory_space=pltpu.SMEM)] + [whole] * len(values),
        out_specs=[whole, whole],
        out_shape=[shape, shape],
    )(coefs, *values)


def on_device(tokens, w_gate, w_up, w_down, pick_block, pick_live, combine_weight):
    experts = lax.axis_size("expert")
    chips = lax.axis_size("dp") // 2
    features = tokens.shape[1]
    model_width = features * experts
    here = tokens.shape[0] // BLOCK
    row_index = lax.axis_index("dp")
    my_expert = lax.axis_index("expert")
    half_bit = row_index % 2
    pair_index = row_index // 2
    offsets = jnp.arange(experts, dtype=jnp.int32) ^ my_expert
    groups = GROUPS if experts == 4 else tuple((d,) for d in range(experts))

    picked = lax.dynamic_index_in_dim(pick_block, pair_index, axis=1, keepdims=False)[offsets]
    live = lax.dynamic_index_in_dim(pick_live, pair_index, axis=1, keepdims=False)[offsets]
    weight = lax.dynamic_index_in_dim(combine_weight, pair_index, axis=1, keepdims=False)[offsets]
    sources = jnp.bitwise_xor(picked // here, half_bit) * here + picked % here

    halves = tokens.reshape(here, 2, HALF, features)
    mine = lax.dynamic_index_in_dim(halves, half_bit, axis=1, keepdims=False)
    theirs = lax.dynamic_index_in_dim(halves, 1 - half_bit, axis=1, keepdims=False)
    other = exchange(theirs, "dp", 1)
    chosen = select(sources, live, mine, other, experts)

    arrived = [chosen[d] if d == 0 else exchange(chosen[d], "expert", d) for d in range(experts)]
    pieces = []
    for d in range(experts):
        gathered = gather_pieces(arrived[d], chips)
        pieces.append((gathered, exchange(gathered, "dp", 1)))
    carry = None
    for g, group in enumerate(groups):
        carry = gate_up(
            offsets[group[0] : group[-1] + 1],
            [pieces[d] for d in group],
            w_gate,
            w_up,
            carry,
            g == len(groups) - 1,
            model_width,
        )
    hidden = carry

    outputs = [None] * experts
    for d in range(experts - 1, -1, -1):
        kept, sent = down(offsets[d : d + 1], hidden, w_down, features)
        received = exchange(sent, "dp", 1)
        sums = add_rounded(kept, received).reshape(chips, HALF, features)
        total = scatter_pieces([sums[j] for j in range(chips)], chips)
        outputs[d] = total if d == 0 else exchange(total, "expert", d)

    slots = jnp.arange(2 * here, dtype=jnp.int32)
    coefs = jnp.where(
        (sources[:, None] == slots[None, :]) & (live[:, None] == 1), weight[:, None], jnp.zeros((), jnp.float32)
    )
    kept, sent = combine(coefs, outputs, here)
    received = exchange(sent, "dp", 1)
    first = jnp.where(half_bit == 0, kept, received)
    second = jnp.where(half_bit == 0, received, kept)
    return jnp.stack([first, second], axis=1).reshape(here * BLOCK, features)


def solution(mesh):
    in_specs = (
        P("dp", "expert"),
        P("expert", None, "dp"),
        P("expert", None, "dp"),
        P("expert", "dp", None),
        P(),
        P(),
        P(),
    )
    out_specs = P("dp", "expert")
    return jax.shard_map(
        on_device, mesh=mesh, in_specs=in_specs, out_specs=out_specs, check_vma=False
    )
```

```python
import functools

import jax
import jax.numpy as jnp
from jax import lax
from jax.experimental import pallas as pl
from jax.experimental.pallas import tpu as pltpu
from jax.sharding import PartitionSpec as P

BLOCK = 128
HALF = BLOCK // 2
MIB = 1024 * 1024
UP_GROUPS = ((0, 1), (2, 3))
DOWN_GROUPS = ((3,), (2,), (1,), (0,))
VMEM = pl.BlockSpec(memory_space=pltpu.VMEM)
SMEM = pl.BlockSpec(memory_space=pltpu.SMEM)
ANY = pl.BlockSpec(memory_space=pl.ANY)
HBM = pl.BlockSpec(memory_space=pltpu.HBM)


def in_hbm(value):
    return pltpu.with_memory_space_constraint(value, pltpu.HBM)


def params(mib):
    return pltpu.CompilerParams(vmem_limit_bytes=mib * MIB)


def exchange(value, axis, offset):
    count = lax.axis_size(axis)
    return lax.ppermute(value, axis, [(i, i ^ offset) for i in range(count)])


def hop(value, step, steps):
    count = lax.axis_size("dp")
    turn = [i ^ (2 << (step if i % 2 == 0 else steps - 1 - step)) for i in range(count)]
    return lax.ppermute(value, "dp", list(enumerate(turn)))


def hop_and_join(value, step, steps):
    return jnp.concatenate([value, hop(value, step, steps)], axis=0)


def after(value, *others):
    return lax.optimization_barrier((value,) + others)[0]


def as_f32(value):
    return value.astype(jnp.float32)


def upper_rows(terms):
    rows = terms[0].shape[0] // 2
    return sum(as_f32(term[rows:]) for term in terms).astype(jnp.bfloat16)


def lower_rows(terms):
    return [term[: term.shape[0] // 2] for term in terms]


def select_kernel(count, pick_block, pick_live, mine, other, *outs):
    here = mine.shape[0] // BLOCK
    expert = lax.axis_index("expert")
    row = lax.axis_index("dp")
    half = row % 2
    for c in range(count):
        picked = pick_block[expert ^ c, row // 2]
        live = pick_live[expert ^ c, row // 2] == 1
        rows = pl.ds(pl.multiple_of((picked % here) * BLOCK + half * HALF, HALF), HALF)
        near = picked // here == half

        @pl.when(live & near)
        def _():
            outs[c][...] = mine[rows, :]

        @pl.when(live & jnp.logical_not(near))
        def _():
            outs[c][...] = other[rows, :]

        @pl.when(jnp.logical_not(live))
        def _():
            outs[c][...] = jnp.zeros_like(outs[c])


def select(pick_block, pick_live, mine, other, count):
    shape = jax.ShapeDtypeStruct((HALF, mine.shape[1]), jnp.bfloat16)
    return pl.pallas_call(
        functools.partial(select_kernel, count),
        in_specs=[SMEM, SMEM, VMEM, VMEM],
        out_specs=[VMEM] * count,
        out_shape=[shape] * count,
        compiler_params=params(6),
    )(pick_block, pick_live, mine, other)


def marker_kernel(*refs):
    refs[-1][...] = jnp.zeros_like(refs[-1])


def marker(flops, *values):
    return pl.pallas_call(
        marker_kernel,
        in_specs=[ANY] * len(values),
        out_specs=VMEM,
        out_shape=jax.ShapeDtypeStruct((8, 128), jnp.float32),
        cost_estimate=pl.CostEstimate(flops=flops, bytes_accessed=0, transcendentals=0),
        compiler_params=params(1),
    )(*values)


def gate_kernel(*refs):
    pass


def gate(value, *others):
    return pl.pallas_call(
        gate_kernel,
        in_specs=[ANY] * (1 + len(others)),
        out_specs=ANY,
        out_shape=jax.ShapeDtypeStruct(value.shape, value.dtype),
        input_output_aliases={0: 0},
        cost_estimate=pl.CostEstimate(flops=0, bytes_accessed=0, transcendentals=0),
        compiler_params=params(1),
    )(value, *others)


def row_copies(offset, place, features, weight, out, sem):
    begin = pl.multiple_of((lax.axis_index("expert") ^ offset) * features, features)
    target = out.at[pl.ds(place * features, features)]
    return [pltpu.make_async_copy(weight.at[0, pl.ds(begin, features)], target, sem)]


def fetch_kernel(group, features, weight, out, sem):
    copies = []
    for c, offset in enumerate(group):
        copies += row_copies(offset, c, features, weight, out, sem.at[c])
    for copy in copies:
        copy.start()
    for copy in copies:
        copy.wait()


def fetch_rows(group, weight, features):
    rows = len(group) * features
    hid = weight.shape[2]
    return pl.pallas_call(
        functools.partial(fetch_kernel, group, features),
        in_specs=[HBM],
        out_specs=VMEM,
        out_shape=pltpu.VMEM((rows, hid), jnp.bfloat16),
        scratch_shapes=[pltpu.SemaphoreType.DMA((len(group),))],
        cost_estimate=pl.CostEstimate(flops=0, bytes_accessed=0, transcendentals=0),
        compiler_params=params(4),
    )(in_hbm(weight))


def gate_up_kernel(count, parts, first, last, model_width, *refs):
    sources, (w_gate, w_up), refs = refs[: 2 * parts], refs[2 * parts : 2 * parts + 2], refs[2 * parts + 2 :]
    features = sources[0].shape[1]
    if not first:
        gate_in, up_in, squares_in = refs[:3]
        refs = refs[3:]
    if last:
        hidden_out, xs, squares = refs
    else:
        gate_out, up_out, squares, xs = refs
    total = jnp.zeros((xs.shape[0], 1), jnp.float32)
    for c in range(count):
        columns = slice(c * features, (c + 1) * features)
        place = 0
        for source in sources:
            for j in range(source.shape[0] // (count * HALF)):
                begin = (j * count + c) * HALF
                xs[place : place + HALF, columns] = source[begin : begin + HALF, :]
                place += HALF
        values = as_f32(xs[:, columns])
        total = total + jnp.sum(values * values, axis=1, keepdims=True)
    total = jnp.broadcast_to(total, squares.shape)
    squares[...] = total if first else total + squares_in[...]
    if last:
        inv_rms = lax.rsqrt(squares[:, :1] / model_width + 1e-05)
    hid = w_gate.shape[1]
    block = next(size for size in (256, 128) if hid % size == 0)

    for b in range(hid // block):
        cols = slice(b * block, (b + 1) * block)
        gate = None if first else gate_in[:, cols]
        up = None if first else up_in[:, cols]
        for c in range(count):
            part = xs[:, c * features : (c + 1) * features]
            rows = slice(c * features, (c + 1) * features)
            dot_gate = jnp.dot(part, w_gate[rows, cols], preferred_element_type=jnp.float32)
            dot_up = jnp.dot(part, w_up[rows, cols], preferred_element_type=jnp.float32)
            gate = dot_gate if gate is None else gate + dot_gate
            up = dot_up if up is None else up + dot_up
        if last:
            gate = gate * inv_rms
            hidden_out[:, cols] = (gate / (1.0 + jnp.exp(-gate)) * (up * inv_rms)).astype(jnp.bfloat16)
        else:
            gate_out[:, cols] = gate
            up_out[:, cols] = up


def gate_up(count, mine, theirs, gate_rows, up_rows, carry, last, model_width):
    first = carry is None
    features = mine[0].shape[1]
    rows = sum(part.shape[0] for part in mine + theirs) // count
    hid = gate_rows.shape[1]
    acc = pltpu.VMEM((rows, hid), jnp.float32)
    scratch = [pltpu.VMEM((rows, count * features), jnp.bfloat16)]
    operands = mine + theirs + [gate_rows, up_rows] + list(carry or ())
    if last:
        out_shape = jax.ShapeDtypeStruct((rows, hid), jnp.bfloat16)
        scratch.append(pltpu.VMEM((rows, 128), jnp.float32))
    else:
        out_shape = [acc, acc, pltpu.VMEM((rows, 128), jnp.float32)]
    return pl.pallas_call(
        functools.partial(gate_up_kernel, count, len(mine), first, last, model_width),
        in_specs=[VMEM] * len(operands),
        out_specs=VMEM if last else [VMEM] * 3,
        out_shape=out_shape,
        scratch_shapes=scratch,
        input_output_aliases={} if first or last else {len(operands) - 3 + i: i for i in range(3)},
        cost_estimate=pl.CostEstimate(
            flops=4 * rows * features * count * hid,
            bytes_accessed=4 * features * count * hid,
            transcendentals=0,
        ),
        compiler_params=params(8),
    )(*operands)


def down_kernel(group, features, hidden, weight, mine, other):
    half = mine.shape[0] // len(group)
    expert = lax.axis_index("expert")
    block = next(size for size in (512, 256, 128) if features % size == 0)
    for c, offset in enumerate(group):
        for b in range(features // block):
            begin = pl.multiple_of((expert ^ offset) * features + b * block, block)
            value = jnp.dot(hidden[...], weight[0, :, pl.ds(begin, block)], preferred_element_type=jnp.float32)
            value = value.astype(jnp.bfloat16)
            cols = slice(c * features + b * block, c * features + (b + 1) * block)
            mine[:, cols] = value[:half]
            other[:, cols] = value[half:]


def down(group, hidden, w_down, features):
    rows, hid = hidden.shape
    width = len(group) * features
    shape = jax.ShapeDtypeStruct((rows // 2, width), jnp.bfloat16)
    return pl.pallas_call(
        functools.partial(down_kernel, group, features),
        in_specs=[VMEM, VMEM],
        out_specs=[VMEM, VMEM],
        out_shape=[shape, shape],
        cost_estimate=pl.CostEstimate(
            flops=2 * rows * hid * width, bytes_accessed=2 * hid * width, transcendentals=0
        ),
        compiler_params=params(8),
    )(hidden, w_down)


def combine_kernel(count, here, pick_block, pick_live, combine_weight, *refs):
    values = refs[:count]
    mine, other = refs[count:]
    expert = lax.axis_index("expert")
    row = lax.axis_index("dp")
    pair = row // 2
    half = row % 2
    for b in range(2 * here):
        slot = (half if b < here else 1 - half) * here + b % here
        total = None
        for c in range(count):
            taken = (pick_live[expert ^ c, pair] == 1) & (pick_block[expert ^ c, pair] == slot)
            coef = jnp.where(taken, combine_weight[expert ^ c, pair], jnp.float32(0))
            term = coef * as_f32(values[c][...])
            total = term if total is None else total + term
        target = mine if b < here else other
        target[b % here] = total.astype(jnp.bfloat16)


def combine(pick_block, pick_live, combine_weight, values, here):
    shape = jax.ShapeDtypeStruct((here,) + values[0].shape, jnp.bfloat16)
    return pl.pallas_call(
        functools.partial(combine_kernel, len(values), here),
        in_specs=[SMEM] * 3 + [VMEM] * len(values),
        out_specs=[VMEM, VMEM],
        out_shape=[shape, shape],
        compiler_params=params(6),
    )(pick_block, pick_live, combine_weight, *values)


def assemble_kernel(kept, received, out):
    half = lax.axis_index("dp") % 2
    for b in range(kept.shape[0]):
        out[pl.ds(pl.multiple_of(b * BLOCK + half * HALF, HALF), HALF), :] = kept[b]
        out[pl.ds(pl.multiple_of(b * BLOCK + (1 - half) * HALF, HALF), HALF), :] = received[b]


def assemble(kept, received):
    here, _, features = kept.shape
    return pl.pallas_call(
        assemble_kernel,
        in_specs=[VMEM, VMEM],
        out_specs=VMEM,
        out_shape=jax.ShapeDtypeStruct((here * BLOCK, features), jnp.bfloat16),
        compiler_params=params(6),
    )(kept, received)


def on_device(tokens, w_gate, w_up, w_down, pick_block, pick_live, combine_weight):
    experts = lax.axis_size("expert")
    steps = (lax.axis_size("dp") // 2).bit_length() - 1
    features = tokens.shape[1]
    model_width = features * experts
    here = tokens.shape[0] // BLOCK
    up_groups = UP_GROUPS if experts == 4 else tuple((d, d + 1) for d in range(0, experts, 2))
    down_groups = DOWN_GROUPS if experts == 4 else tuple((d,) for d in range(experts - 1, -1, -1))

    chosen = select(pick_block, pick_live, tokens, exchange(tokens, "dp", 1), experts)
    arrived = [chosen[d] if d == 0 else exchange(chosen[d], "expert", d) for d in range(experts)]
    own = [jnp.concatenate([arrived[d] for d in group], axis=0) for group in up_groups]
    token = marker(3000000000, *(arrived[d] for group in up_groups[1:] for d in group))
    gate_rows, up_rows, joined, mine, theirs = [], [], [], [], []
    for g, group in enumerate(up_groups):
        if g == 0:
            gate_rows.append(fetch_rows(group, after(w_gate, chosen[0]), features))
            own[g] = after(own[g], gate_rows[g])
        up_rows.append(fetch_rows(group, after(w_up, own[g], *joined[-1:]), features))
        if g + 1 < len(up_groups):
            gate_rows.append(fetch_rows(up_groups[g + 1], after(w_gate, up_rows[g]), features))
        value = own[g]
        for step in range(steps - 1):
            value = hop_and_join(value, step, steps)
        if g == 0:
            value = gate(value, token)
        joined.append(after(value, up_rows[g], gate_rows[-1]))
    for g in range(len(up_groups)):
        last_hop = hop(joined[g], steps - 1, steps)
        if g + 1 < len(up_groups):
            whole = jnp.concatenate([joined[g], last_hop], axis=0)
            whole = after(whole, joined[g + 1])
            mine.append([whole])
            theirs.append([exchange(whole, "dp", 1)])
        else:
            mine.append([joined[g], last_hop])
            theirs.append([exchange(joined[g], "dp", 1)])
    carry = None
    for g, group in enumerate(up_groups):
        last = g == len(up_groups) - 1
        if last:
            mine[g][1] = after(mine[g][1], carry[2])
            theirs[g].append(exchange(mine[g][1], "dp", 1))
        carry = gate_up(len(group), mine[g], theirs[g], gate_rows[g], up_rows[g], carry, last, model_width)
    hidden = carry

    terms, firsts = [], []
    for i, group in enumerate(down_groups):
        ready = hidden if i < 2 else after(hidden, firsts[i - 2])
        kept, sent = down(group, ready, w_down, features)
        terms.append([kept, exchange(sent, "dp", 1)])
        firsts.append(upper_rows(terms[i]))
    outputs = [None] * experts
    for i, group in enumerate(down_groups):
        sent = firsts[i]
        for step in range(steps - 1, -1, -1):
            if step < steps - 1:
                sent = upper_rows(terms[i])
                if step == 0 and i + 2 < len(firsts):
                    sent = after(sent, firsts[i + 2])
            terms[i] = lower_rows(terms[i]) + [hop(sent, step, steps)]
        total = sum(as_f32(term) for term in terms[i]).astype(jnp.bfloat16)
        for c, d in enumerate(group):
            value = total[:, c * features : (c + 1) * features]
            outputs[d] = value if d == 0 else exchange(value, "expert", d)

    kept, sent = combine(pick_block, pick_live, combine_weight, outputs, here)
    return assemble(kept, exchange(sent, "dp", 1))


def solution(mesh):
    in_specs = (
        P("dp", "expert"),
        P("expert", None, "dp"),
        P("expert", None, "dp"),
        P("expert", "dp", None),
        P(),
        P(),
        P(),
    )
    out_specs = P("dp", "expert")
    return jax.shard_map(
        on_device, mesh=mesh, in_specs=in_specs, out_specs=out_specs, check_vma=False
    )
```

```python
import functools

import jax
import jax.numpy as jnp
from jax import lax
from jax.experimental import pallas as pl
from jax.experimental.pallas import tpu as pltpu
from jax.sharding import PartitionSpec as P

BLOCK = 128
HALF = BLOCK // 2
MIB = 1024 * 1024
UP_GROUPS = ((0, 1), (2, 3))
DOWN_ORDER = (
    ("o3",), ("m3", "o2"), ("h3",), ("m2", "o1"), ("h2",), ("m1", "o0", "m0"), ("h3",), ("h1",), ("h2",),
    ("h0",), ("f3",), ("f2",), ("h1",), ("h0",), ("f1",), ("f0",),
)
VMEM = pl.BlockSpec(memory_space=pltpu.VMEM)
SMEM = pl.BlockSpec(memory_space=pltpu.SMEM)
ANY = pl.BlockSpec(memory_space=pl.ANY)
HBM = pl.BlockSpec(memory_space=pltpu.HBM)


def in_hbm(value):
    return pltpu.with_memory_space_constraint(value, pltpu.HBM)


def params(mib):
    return pltpu.CompilerParams(vmem_limit_bytes=mib * MIB)


def exchange(value, axis, offset):
    count = lax.axis_size(axis)
    return lax.ppermute(value, axis, [(i, i ^ offset) for i in range(count)])


def hop(value, step, steps):
    count = lax.axis_size("dp")
    turn = [i ^ (2 << (step if i % 2 == 0 else steps - 1 - step)) for i in range(count)]
    return lax.ppermute(value, "dp", list(enumerate(turn)))


def hop_and_join(value, step, steps):
    return jnp.concatenate([value, hop(value, step, steps)], axis=0)


def after(value, *others):
    return lax.optimization_barrier((value,) + others)[0]


def as_f32(value):
    return value.astype(jnp.float32)


def upper_rows(terms):
    rows = terms[0].shape[0] // 2
    return sum(as_f32(term[rows:]) for term in terms).astype(jnp.bfloat16)


def lower_rows(terms):
    return [term[: term.shape[0] // 2] for term in terms]


def plan_kernel(count, pick_block, pick_live, tokens, near, mask, blocks, picked, live, block_sem, sem):
    here = tokens.shape[0] // BLOCK
    expert = lax.axis_index("expert")
    row = lax.axis_index("dp")
    half = row % 2
    loads = []
    for b in range(here):
        rows = pl.ds(pl.multiple_of(b * BLOCK + half * HALF, HALF), HALF)
        loads.append(pltpu.make_async_copy(tokens.at[rows], blocks.at[b], block_sem.at[b]))
    loads.append(pltpu.make_async_copy(pick_block, picked, sem.at[0]))
    loads.append(pltpu.make_async_copy(pick_live, live, sem.at[1]))
    for load in loads:
        load.start()
    for load in loads:
        load.wait()
    for c in range(count):
        slot = picked[expert ^ c, row // 2]
        taken = live[expert ^ c, row // 2] == 1
        held = taken & (slot // here == half)
        value = jnp.zeros(near.shape[1:], jnp.float32)
        for b in range(here):
            keep = jnp.where(held & (slot % here == b), jnp.float32(1), jnp.float32(0))
            value = value + keep * as_f32(blocks[b])
            away = taken & (slot // here != half) & (slot % here == b)
            mask[c * here + b] = jnp.full(mask.shape[1:], jnp.where(away, jnp.float32(1), jnp.float32(0)))
        near[c] = value.astype(jnp.bfloat16)


def plan(pick_block, pick_live, tokens, count):
    here = tokens.shape[0] // BLOCK
    features = tokens.shape[1]
    return pl.pallas_call(
        functools.partial(plan_kernel, count),
        in_specs=[HBM] * 3,
        out_specs=[VMEM, VMEM],
        out_shape=[
            jax.ShapeDtypeStruct((count, HALF, features), jnp.bfloat16),
            jax.ShapeDtypeStruct((count * here, 8, 128), jnp.float32),
        ],
        scratch_shapes=[
            pltpu.VMEM((here, HALF, features), jnp.bfloat16),
            pltpu.SMEM(pick_block.shape, pick_block.dtype),
            pltpu.SMEM(pick_live.shape, pick_live.dtype),
            pltpu.SemaphoreType.DMA((here,)),
            pltpu.SemaphoreType.DMA((2,)),
        ],
        cost_estimate=pl.CostEstimate(flops=0, bytes_accessed=0, transcendentals=0),
        compiler_params=params(6),
    )(in_hbm(pick_block), in_hbm(pick_live), in_hbm(tokens))


def select_kernel(count, near, mask, other, *outs):
    here = other.shape[0] // BLOCK
    half = lax.axis_index("dp") % 2
    blocks = []
    for b in range(here):
        rows = pl.ds(pl.multiple_of(b * BLOCK + half * HALF, HALF), HALF)
        blocks.append(as_f32(other[rows, :]))
    for c in range(count):
        value = as_f32(near[c])
        for b in range(here):
            value = value + mask[c * here + b, 0:1, 0:1] * blocks[b]
        outs[c][...] = value.astype(jnp.bfloat16)


def select(near, mask, other, count):
    shape = jax.ShapeDtypeStruct((HALF, other.shape[1]), jnp.bfloat16)
    return pl.pallas_call(
        functools.partial(select_kernel, count),
        in_specs=[VMEM] * 3,
        out_specs=[VMEM] * count,
        out_shape=[shape] * count,
        compiler_params=params(6),
    )(near, mask, other)


def marker_kernel(*refs):
    refs[-1][...] = jnp.zeros_like(refs[-1])


def marker(flops, *values):
    return pl.pallas_call(
        marker_kernel,
        in_specs=[ANY] * len(values),
        out_specs=VMEM,
        out_shape=jax.ShapeDtypeStruct((8, 128), jnp.float32),
        cost_estimate=pl.CostEstimate(flops=flops, bytes_accessed=0, transcendentals=0),
        compiler_params=params(1),
    )(*values)


def gate_kernel(*refs):
    pass


def gate(value, *others):
    return pl.pallas_call(
        gate_kernel,
        in_specs=[ANY] * (1 + len(others)),
        out_specs=ANY,
        out_shape=jax.ShapeDtypeStruct(value.shape, value.dtype),
        input_output_aliases={0: 0},
        cost_estimate=pl.CostEstimate(flops=0, bytes_accessed=0, transcendentals=0),
        compiler_params=params(1),
    )(value, *others)


def row_copies(offset, place, features, weight, out, sem):
    begin = pl.multiple_of((lax.axis_index("expert") ^ offset) * features, features)
    target = out.at[pl.ds(place * features, features)]
    return [pltpu.make_async_copy(weight.at[0, pl.ds(begin, features)], target, sem)]


def fetch_kernel(group, features, weight, out, sem):
    copies = []
    for c, offset in enumerate(group):
        copies += row_copies(offset, c, features, weight, out, sem.at[c])
    for copy in copies:
        copy.start()
    for copy in copies:
        copy.wait()


def fetch_rows(group, weight, features):
    rows = len(group) * features
    hid = weight.shape[2]
    return pl.pallas_call(
        functools.partial(fetch_kernel, group, features),
        in_specs=[HBM],
        out_specs=VMEM,
        out_shape=pltpu.VMEM((rows, hid), jnp.bfloat16),
        scratch_shapes=[pltpu.SemaphoreType.DMA((len(group),))],
        cost_estimate=pl.CostEstimate(flops=0, bytes_accessed=0, transcendentals=0),
        compiler_params=params(4),
    )(in_hbm(weight))


def gate_up_kernel(count, first, place, model_width, mine, theirs, w_gate, w_up, *refs):
    last = place is not None
    if not first:
        gate_in, up_in, squares_in = refs[:3]
        refs = refs[3:]
    if last:
        hidden_out, xs, squares = refs[-3:]
    else:
        gate_out, up_out, squares, xs = refs
    features = mine.shape[1]
    half = xs.shape[0] // 2
    total = jnp.zeros((2 * half, 1), jnp.float32)
    for c in range(count):
        columns = slice(c * features, (c + 1) * features)
        for k, source in enumerate((mine, theirs)):
            for j in range(half // HALF):
                begin = (j * count + c) * HALF
                xs[k * half + j * HALF : k * half + (j + 1) * HALF, columns] = source[begin : begin + HALF, :]
        values = as_f32(xs[:, columns])
        total = total + jnp.sum(values * values, axis=1, keepdims=True)
    total = jnp.broadcast_to(total, squares.shape)
    squares[...] = total if first else total + squares_in[...]
    if last:
        inv_rms = lax.rsqrt(squares[:, :1] / model_width + 1e-05)
    hid = w_gate.shape[1]
    block = next(size for size in (256, 128) if hid % size == 0)

    for b in range(hid // block):
        cols = slice(b * block, (b + 1) * block)
        gate = None if first else gate_in[:, cols]
        up = None if first else up_in[:, cols]
        for c in range(count):
            part = xs[:, c * features : (c + 1) * features]
            rows = slice(c * features, (c + 1) * features)
            dot_gate = jnp.dot(part, w_gate[rows, cols], preferred_element_type=jnp.float32)
            dot_up = jnp.dot(part, w_up[rows, cols], preferred_element_type=jnp.float32)
            gate = dot_gate if gate is None else gate + dot_gate
            up = dot_up if up is None else up + dot_up
        if last:
            gate = gate * inv_rms
            value = (gate / (1.0 + jnp.exp(-gate)) * (up * inv_rms)).astype(jnp.bfloat16)
            hidden_out[place * half : (place + 1) * half, cols] = value[:half]
            hidden_out[(2 + place) * half : (3 + place) * half, cols] = value[half:]
        else:
            gate_out[:, cols] = gate
            up_out[:, cols] = up


def gate_up(count, mine, theirs, gate_rows, up_rows, carry, place, hidden, model_width):
    first = carry is None
    features = mine.shape[1]
    rows = 2 * mine.shape[0] // count
    hid = gate_rows.shape[1]
    acc = pltpu.VMEM((rows, hid), jnp.float32)
    scratch = [pltpu.VMEM((rows, count * features), jnp.bfloat16)]
    operands = [mine, theirs, gate_rows, up_rows] + list(carry or ())
    in_specs = [VMEM] * len(operands)
    aliases = {}
    if place is not None:
        out_shape = [pltpu.VMEM((2 * rows, hid), jnp.bfloat16)]
        scratch.append(pltpu.VMEM((rows, 128), jnp.float32))
        if hidden is not None:
            aliases = {len(operands): 0}
            operands.append(hidden)
            in_specs.append(ANY)
    else:
        out_shape = [acc, acc, pltpu.VMEM((rows, 128), jnp.float32)]
        if not first:
            aliases = {4: 0, 5: 1, 6: 2}
    return pl.pallas_call(
        functools.partial(gate_up_kernel, count, first, place, model_width),
        in_specs=in_specs,
        out_specs=[VMEM] * len(out_shape),
        out_shape=out_shape,
        scratch_shapes=scratch,
        input_output_aliases=aliases,
        cost_estimate=pl.CostEstimate(
            flops=4 * rows * features * count * hid,
            bytes_accessed=4 * features * count * hid,
            transcendentals=0,
        ),
        compiler_params=params(8),
    )(*operands)


def down_kernel(parts, hidden, weight, *outs):
    for (kind, offset), out in zip(parts, outs):
        rows, features = out.shape
        first_row = rows if kind == "o" else 0
        block = next(size for size in (512, 256, 128) if features % size == 0)
        for b in range(features // block):
            begin = pl.multiple_of((lax.axis_index("expert") ^ offset) * features + b * block, block)
            value = jnp.dot(
                hidden[first_row : first_row + rows, :],
                weight[0, :, pl.ds(begin, block)],
                preferred_element_type=jnp.float32,
            )
            out[:, b * block : (b + 1) * block] = value.astype(jnp.bfloat16)


def down(parts, hidden, w_down, features):
    rows = hidden.shape[0] // 2
    return pl.pallas_call(
        functools.partial(down_kernel, parts),
        in_specs=[VMEM, VMEM],
        out_specs=[VMEM] * len(parts),
        out_shape=[jax.ShapeDtypeStruct((rows, features), jnp.bfloat16)] * len(parts),
        cost_estimate=pl.CostEstimate(flops=0, bytes_accessed=0, transcendentals=0),
        compiler_params=params(8),
    )(hidden, w_down)


def combine_kernel(count, here, pick_block, pick_live, combine_weight, *refs):
    values = refs[:count]
    mine, other = refs[count:]
    expert = lax.axis_index("expert")
    row = lax.axis_index("dp")
    pair = row // 2
    half = row % 2
    for b in range(2 * here):
        slot = (half if b < here else 1 - half) * here + b % here
        total = None
        for c in range(count):
            taken = (pick_live[expert ^ c, pair] == 1) & (pick_block[expert ^ c, pair] == slot)
            coef = jnp.where(taken, combine_weight[expert ^ c, pair], jnp.float32(0))
            term = coef * as_f32(values[c][...])
            total = term if total is None else total + term
        target = mine if b < here else other
        target[b % here] = total.astype(jnp.bfloat16)


def combine(pick_block, pick_live, combine_weight, values, here):
    shape = jax.ShapeDtypeStruct((here,) + values[0].shape, jnp.bfloat16)
    return pl.pallas_call(
        functools.partial(combine_kernel, len(values), here),
        in_specs=[SMEM] * 3 + [VMEM] * len(values),
        out_specs=[VMEM, VMEM],
        out_shape=[shape, shape],
        compiler_params=params(6),
    )(pick_block, pick_live, combine_weight, *values)


def assemble_kernel(kept, received, out):
    half = lax.axis_index("dp") % 2
    for b in range(kept.shape[0]):
        out[pl.ds(pl.multiple_of(b * BLOCK + half * HALF, HALF), HALF), :] = kept[b]
        out[pl.ds(pl.multiple_of(b * BLOCK + (1 - half) * HALF, HALF), HALF), :] = received[b]


def assemble(kept, received):
    here, _, features = kept.shape
    return pl.pallas_call(
        assemble_kernel,
        in_specs=[VMEM, VMEM],
        out_specs=VMEM,
        out_shape=jax.ShapeDtypeStruct((here * BLOCK, features), jnp.bfloat16),
        compiler_params=params(6),
    )(kept, received)


def on_device(tokens, w_gate, w_up, w_down, pick_block, pick_live, combine_weight):
    experts = lax.axis_size("expert")
    steps = (lax.axis_size("dp") // 2).bit_length() - 1
    features = tokens.shape[1]
    model_width = features * experts
    here = tokens.shape[0] // BLOCK
    up_groups = UP_GROUPS if experts == 4 else tuple((d, d + 1) for d in range(0, experts, 2))

    near, mask = plan(pick_block, pick_live, tokens, experts)
    chosen = select(near, mask, exchange(tokens, "dp", 1), experts)
    arrived = [chosen[d] if d == 0 else exchange(chosen[d], "expert", d) for d in range(experts)]
    own = [jnp.concatenate([arrived[d] for d in group], axis=0) for group in up_groups]
    token = marker(3000000000, *(arrived[d] for group in up_groups[1:] for d in group))
    gate_rows, up_rows, joined, mine, theirs = [], [], [], [], []
    for g, group in enumerate(up_groups):
        if g == 0:
            gate_rows.append(fetch_rows(group, after(w_gate, chosen[0]), features))
            own[g] = after(own[g], gate_rows[g])
        if g != 1:
            up_rows.append(fetch_rows(group, after(w_up, own[g], *joined[-1:]), features))
        if g + 1 < len(up_groups):
            gate_rows.append(fetch_rows(up_groups[g + 1], after(w_gate, up_rows[-1]), features))
        value = own[g]
        for step in range(steps - 2):
            value = hop_and_join(value, step, steps)
        received = hop(value, steps - 2, steps)
        if g == 0:
            value = gate(value, token)
        if g != 1:
            value = jnp.concatenate([value, received], axis=0)
        if g == 0:
            value = after(value, up_rows[0], gate_rows[-1])
        elif g == 1:
            near_theirs = exchange(joined[0], "dp", 1)
            near = after(joined[0], own[1])
            near_sums = gate_up(
                len(up_groups[0]), near, near_theirs, gate_rows[0], up_rows[0], None, None, None, model_width
            )
            up_rows.append(fetch_rows(group, after(w_up, near_sums[2]), features))
            value = jnp.concatenate([value, after(received, up_rows[1])], axis=0)
        joined.append(value)
    far = [hop(value, steps - 1, steps) for value in joined]
    far[0] = after(far[0], joined[1])
    far_sums = None
    for g, group in enumerate(up_groups):
        last = g == len(up_groups) - 1
        weights = (gate_rows[g], up_rows[g])
        if g > 0:
            near_theirs = exchange(joined[g], "dp", 1)
            near = after(joined[g], far_sums[2])
            near_sums = gate_up(
                len(group), near, near_theirs, *weights, near_sums, 0 if last else None, None, model_width
            )
        rows = after(far[g], near_sums[-1])
        hidden = near_sums[0] if last else None
        far_theirs = exchange(rows, "dp", 1)
        far_sums = gate_up(
            len(group), rows, far_theirs, *weights, far_sums, 1 if last else None, hidden, model_width
        )
    hidden = far_sums[0]

    if experts == 4 and steps == 2:
        order = DOWN_ORDER
    else:
        order = [(kind + str(d),) for d in range(experts - 1, -1, -1) for kind in ["o", "m"] + ["h"] * steps + ["f"]]
    terms = [[] for _ in range(experts)]
    hops = [0] * experts
    outputs = [None] * experts
    done = hidden
    for entry in order:
        parts = tuple((part[0], int(part[1:])) for part in entry)
        if parts[0][0] in "om":
            for (kind, d), value in zip(parts, down(parts, after(hidden, done), w_down, features)):
                done = value
                terms[d].append(exchange(done, "dp", 1) if kind == "o" else done)
            continue
        kind, d = parts[0]
        terms[d][-1] = after(terms[d][-1], done)
        if kind == "h":
            hops[d] += 1
            done = upper_rows(terms[d])
            terms[d] = lower_rows(terms[d]) + [hop(done, steps - hops[d], steps)]
        else:
            done = sum(as_f32(term) for term in terms[d]).astype(jnp.bfloat16)
            outputs[d] = done if d == 0 else exchange(done, "expert", d)

    kept, sent = combine(pick_block, pick_live, combine_weight, outputs, here)
    return assemble(kept, exchange(sent, "dp", 1))


def solution(mesh):
    in_specs = (
        P("dp", "expert"),
        P("expert", None, "dp"),
        P("expert", None, "dp"),
        P("expert", "dp", None),
        P(),
        P(),
        P(),
    )
    out_specs = P("dp", "expert")
    return jax.shard_map(
        on_device, mesh=mesh, in_specs=in_specs, out_specs=out_specs, check_vma=False
    )
```

```python
import functools

import jax
import jax.numpy as jnp
from jax import lax
from jax.experimental import pallas as pl
from jax.experimental.pallas import tpu as pltpu
from jax.sharding import PartitionSpec as P

BLOCK = 128
HALF = BLOCK // 2
MIB = 1024 * 1024
UP_GROUPS = ((0, 1), (2, 3))
DOWN_ORDER = (
    ("o3",), ("m3", "o2"), ("h3",), ("m2", "o1"), ("h2",), ("m1", "o0", "m0"), ("h3",), ("h1",), ("h2",),
    ("h0",), ("f3",), ("h1",), ("f2",), ("h0",), ("f1",), ("f0",),
)
VMEM = pl.BlockSpec(memory_space=pltpu.VMEM)
SMEM = pl.BlockSpec(memory_space=pltpu.SMEM)
ANY = pl.BlockSpec(memory_space=pl.ANY)
HBM = pl.BlockSpec(memory_space=pltpu.HBM)


def in_hbm(value):
    return pltpu.with_memory_space_constraint(value, pltpu.HBM)


def params(mib):
    return pltpu.CompilerParams(vmem_limit_bytes=mib * MIB)


def exchange(value, axis, offset):
    count = lax.axis_size(axis)
    return lax.ppermute(value, axis, [(i, i ^ offset) for i in range(count)])


def hop(value, step, steps):
    count = lax.axis_size("dp")
    turn = [i ^ (2 << (step if i % 2 == 0 else steps - 1 - step)) for i in range(count)]
    return lax.ppermute(value, "dp", list(enumerate(turn)))


def hop_and_join(value, step, steps):
    return jnp.concatenate([value, hop(value, step, steps)], axis=0)


def after(value, *others):
    return lax.optimization_barrier((value,) + others)[0]


def as_f32(value):
    return value.astype(jnp.float32)


def upper_rows(terms):
    rows = terms[0].shape[0] // 2
    return sum(as_f32(term[rows:]) for term in terms).astype(jnp.bfloat16)


def lower_rows(terms):
    return [term[: term.shape[0] // 2] for term in terms]


def plan_kernel(count, pick_block, pick_live, tokens, near, mask, blocks, picked, live, block_sem, sem):
    here = tokens.shape[0] // BLOCK
    expert = lax.axis_index("expert")
    row = lax.axis_index("dp")
    half = row % 2
    loads = []
    for b in range(here):
        rows = pl.ds(pl.multiple_of(b * BLOCK + half * HALF, HALF), HALF)
        loads.append(pltpu.make_async_copy(tokens.at[rows], blocks.at[b], block_sem.at[b]))
    loads.append(pltpu.make_async_copy(pick_block, picked, sem.at[0]))
    loads.append(pltpu.make_async_copy(pick_live, live, sem.at[1]))
    for load in loads:
        load.start()
    for load in loads:
        load.wait()
    for c in range(count):
        slot = picked[expert ^ c, row // 2]
        taken = live[expert ^ c, row // 2] == 1
        held = taken & (slot // here == half)
        value = jnp.zeros(near.shape[1:], jnp.float32)
        for b in range(here):
            keep = jnp.where(held & (slot % here == b), jnp.float32(1), jnp.float32(0))
            value = value + keep * as_f32(blocks[b])
            away = taken & (slot // here != half) & (slot % here == b)
            mask[c * here + b] = jnp.full(mask.shape[1:], jnp.where(away, jnp.float32(1), jnp.float32(0)))
        near[c] = value.astype(jnp.bfloat16)


def plan(pick_block, pick_live, tokens, count):
    here = tokens.shape[0] // BLOCK
    features = tokens.shape[1]
    return pl.pallas_call(
        functools.partial(plan_kernel, count),
        in_specs=[HBM] * 3,
        out_specs=[VMEM, VMEM],
        out_shape=[
            jax.ShapeDtypeStruct((count, HALF, features), jnp.bfloat16),
            jax.ShapeDtypeStruct((count * here, 8, 128), jnp.float32),
        ],
        scratch_shapes=[
            pltpu.VMEM((here, HALF, features), jnp.bfloat16),
            pltpu.SMEM(pick_block.shape, pick_block.dtype),
            pltpu.SMEM(pick_live.shape, pick_live.dtype),
            pltpu.SemaphoreType.DMA((here,)),
            pltpu.SemaphoreType.DMA((2,)),
        ],
        cost_estimate=pl.CostEstimate(flops=0, bytes_accessed=0, transcendentals=0),
        compiler_params=params(6),
    )(in_hbm(pick_block), in_hbm(pick_live), in_hbm(tokens))


def select_kernel(count, near, mask, other, *outs):
    here = other.shape[0] // BLOCK
    half = lax.axis_index("dp") % 2
    blocks = []
    for b in range(here):
        rows = pl.ds(pl.multiple_of(b * BLOCK + half * HALF, HALF), HALF)
        blocks.append(as_f32(other[rows, :]))
    for c in range(count):
        value = as_f32(near[c])
        for b in range(here):
            value = value + mask[c * here + b, 0:1, 0:1] * blocks[b]
        outs[c][...] = value.astype(jnp.bfloat16)


def select(near, mask, other, count):
    shape = jax.ShapeDtypeStruct((HALF, other.shape[1]), jnp.bfloat16)
    return pl.pallas_call(
        functools.partial(select_kernel, count),
        in_specs=[VMEM] * 3,
        out_specs=[VMEM] * count,
        out_shape=[shape] * count,
        compiler_params=params(6),
    )(near, mask, other)


def marker_kernel(*refs):
    refs[-1][...] = jnp.zeros_like(refs[-1])


def marker(flops, *values):
    return pl.pallas_call(
        marker_kernel,
        in_specs=[ANY] * len(values),
        out_specs=VMEM,
        out_shape=jax.ShapeDtypeStruct((8, 128), jnp.float32),
        cost_estimate=pl.CostEstimate(flops=flops, bytes_accessed=0, transcendentals=0),
        compiler_params=params(1),
    )(*values)


def gate_kernel(*refs):
    pass


def gate(value, *others):
    return pl.pallas_call(
        gate_kernel,
        in_specs=[ANY] * (1 + len(others)),
        out_specs=ANY,
        out_shape=jax.ShapeDtypeStruct(value.shape, value.dtype),
        input_output_aliases={0: 0},
        cost_estimate=pl.CostEstimate(flops=0, bytes_accessed=0, transcendentals=0),
        compiler_params=params(1),
    )(value, *others)


def row_copies(offset, place, features, weight, out, sem):
    begin = pl.multiple_of((lax.axis_index("expert") ^ offset) * features, features)
    target = out.at[pl.ds(place * features, features)]
    return [pltpu.make_async_copy(weight.at[0, pl.ds(begin, features)], target, sem)]


def fetch_kernel(group, features, weight, out, sem):
    copies = []
    for c, offset in enumerate(group):
        copies += row_copies(offset, c, features, weight, out, sem.at[c])
    for copy in copies:
        copy.start()
    for copy in copies:
        copy.wait()


def fetch_rows(group, weight, features):
    rows = len(group) * features
    hid = weight.shape[2]
    return pl.pallas_call(
        functools.partial(fetch_kernel, group, features),
        in_specs=[HBM],
        out_specs=VMEM,
        out_shape=pltpu.VMEM((rows, hid), jnp.bfloat16),
        scratch_shapes=[pltpu.SemaphoreType.DMA((len(group),))],
        cost_estimate=pl.CostEstimate(flops=0, bytes_accessed=0, transcendentals=0),
        compiler_params=params(4),
    )(in_hbm(weight))


def gate_up_kernel(count, first, place, model_width, mine, theirs, w_gate, w_up, *refs):
    last = place is not None
    if not first:
        gate_in, up_in, squares_in = refs[:3]
        refs = refs[3:]
    if last:
        hidden_out, xs, squares = refs[-3:]
    else:
        gate_out, up_out, squares, xs = refs
    features = mine.shape[1]
    half = xs.shape[0] // 2
    total = jnp.zeros((2 * half, 1), jnp.float32)
    for c in range(count):
        columns = slice(c * features, (c + 1) * features)
        for k, source in enumerate((mine, theirs)):
            for j in range(half // HALF):
                begin = (j * count + c) * HALF
                xs[k * half + j * HALF : k * half + (j + 1) * HALF, columns] = source[begin : begin + HALF, :]
        values = as_f32(xs[:, columns])
        total = total + jnp.sum(values * values, axis=1, keepdims=True)
    total = jnp.broadcast_to(total, squares.shape)
    squares[...] = total if first else total + squares_in[...]
    if last:
        inv_rms = lax.rsqrt(squares[:, :1] / model_width + 1e-05)
    hid = w_gate.shape[1]
    block = next(size for size in (256, 128) if hid % size == 0)

    for b in range(hid // block):
        cols = slice(b * block, (b + 1) * block)
        gate = None if first else gate_in[:, cols]
        up = None if first else up_in[:, cols]
        for c in range(count):
            part = xs[:, c * features : (c + 1) * features]
            rows = slice(c * features, (c + 1) * features)
            dot_gate = jnp.dot(part, w_gate[rows, cols], preferred_element_type=jnp.float32)
            dot_up = jnp.dot(part, w_up[rows, cols], preferred_element_type=jnp.float32)
            gate = dot_gate if gate is None else gate + dot_gate
            up = dot_up if up is None else up + dot_up
        if last:
            gate = gate * inv_rms
            value = (gate / (1.0 + jnp.exp(-gate)) * (up * inv_rms)).astype(jnp.bfloat16)
            hidden_out[place * half : (place + 1) * half, cols] = value[:half]
            hidden_out[(2 + place) * half : (3 + place) * half, cols] = value[half:]
        else:
            gate_out[:, cols] = gate
            up_out[:, cols] = up


def gate_up(count, mine, theirs, gate_rows, up_rows, carry, place, hidden, model_width):
    first = carry is None
    features = mine.shape[1]
    rows = 2 * mine.shape[0] // count
    hid = gate_rows.shape[1]
    acc = pltpu.VMEM((rows, hid), jnp.float32)
    scratch = [pltpu.VMEM((rows, count * features), jnp.bfloat16)]
    operands = [mine, theirs, gate_rows, up_rows] + list(carry or ())
    in_specs = [VMEM] * len(operands)
    aliases = {}
    if place is not None:
        out_shape = [pltpu.VMEM((2 * rows, hid), jnp.bfloat16)]
        scratch.append(pltpu.VMEM((rows, 128), jnp.float32))
        if hidden is not None:
            aliases = {len(operands): 0}
            operands.append(hidden)
            in_specs.append(ANY)
    else:
        out_shape = [acc, acc, pltpu.VMEM((rows, 128), jnp.float32)]
        if not first:
            aliases = {4: 0, 5: 1, 6: 2}
    return pl.pallas_call(
        functools.partial(gate_up_kernel, count, first, place, model_width),
        in_specs=in_specs,
        out_specs=[VMEM] * len(out_shape),
        out_shape=out_shape,
        scratch_shapes=scratch,
        input_output_aliases=aliases,
        cost_estimate=pl.CostEstimate(
            flops=4 * rows * features * count * hid,
            bytes_accessed=4 * features * count * hid,
            transcendentals=0,
        ),
        compiler_params=params(8),
    )(*operands)


def down_kernel(parts, hidden, weight, *outs):
    for (kind, offset), out in zip(parts, outs):
        rows, features = out.shape
        first_row = rows if kind == "o" else 0
        block = next(size for size in (512, 256, 128) if features % size == 0)
        for b in range(features // block):
            begin = pl.multiple_of((lax.axis_index("expert") ^ offset) * features + b * block, block)
            value = jnp.dot(
                hidden[first_row : first_row + rows, :],
                weight[0, :, pl.ds(begin, block)],
                preferred_element_type=jnp.float32,
            )
            out[:, b * block : (b + 1) * block] = value.astype(jnp.bfloat16)


def down(parts, hidden, w_down, features):
    rows = hidden.shape[0] // 2
    return pl.pallas_call(
        functools.partial(down_kernel, parts),
        in_specs=[VMEM, VMEM],
        out_specs=[VMEM] * len(parts),
        out_shape=[jax.ShapeDtypeStruct((rows, features), jnp.bfloat16)] * len(parts),
        cost_estimate=pl.CostEstimate(flops=0, bytes_accessed=0, transcendentals=0),
        compiler_params=params(8),
    )(hidden, w_down)


def combine_kernel(count, here, pick_block, pick_live, combine_weight, *refs):
    values = refs[:count]
    mine, other = refs[count:]
    expert = lax.axis_index("expert")
    row = lax.axis_index("dp")
    pair = row // 2
    half = row % 2
    for b in range(2 * here):
        slot = (half if b < here else 1 - half) * here + b % here
        total = None
        for c in range(count):
            taken = (pick_live[expert ^ c, pair] == 1) & (pick_block[expert ^ c, pair] == slot)
            coef = jnp.where(taken, combine_weight[expert ^ c, pair], jnp.float32(0))
            term = coef * as_f32(values[c][...])
            total = term if total is None else total + term
        target = mine if b < here else other
        target[b % here] = total.astype(jnp.bfloat16)


def combine(pick_block, pick_live, combine_weight, values, here):
    shape = jax.ShapeDtypeStruct((here,) + values[0].shape, jnp.bfloat16)
    return pl.pallas_call(
        functools.partial(combine_kernel, len(values), here),
        in_specs=[SMEM] * 3 + [VMEM] * len(values),
        out_specs=[VMEM, VMEM],
        out_shape=[shape, shape],
        compiler_params=params(6),
    )(pick_block, pick_live, combine_weight, *values)


def assemble_kernel(kept, received, out):
    half = lax.axis_index("dp") % 2
    for b in range(kept.shape[0]):
        out[pl.ds(pl.multiple_of(b * BLOCK + half * HALF, HALF), HALF), :] = kept[b]
        out[pl.ds(pl.multiple_of(b * BLOCK + (1 - half) * HALF, HALF), HALF), :] = received[b]


def assemble(kept, received):
    here, _, features = kept.shape
    return pl.pallas_call(
        assemble_kernel,
        in_specs=[VMEM, VMEM],
        out_specs=VMEM,
        out_shape=jax.ShapeDtypeStruct((here * BLOCK, features), jnp.bfloat16),
        compiler_params=params(6),
    )(kept, received)


def on_device(tokens, w_gate, w_up, w_down, pick_block, pick_live, combine_weight):
    experts = lax.axis_size("expert")
    steps = (lax.axis_size("dp") // 2).bit_length() - 1
    features = tokens.shape[1]
    model_width = features * experts
    here = tokens.shape[0] // BLOCK
    up_groups = UP_GROUPS if experts == 4 else tuple((d, d + 1) for d in range(0, experts, 2))

    near, mask = plan(pick_block, pick_live, tokens, experts)
    chosen = select(near, mask, exchange(tokens, "dp", 1), experts)
    arrived = [chosen[d] if d == 0 else exchange(chosen[d], "expert", d) for d in range(experts)]
    own = [jnp.concatenate([arrived[d] for d in group], axis=0) for group in up_groups]
    token = marker(3000000000, *(arrived[d] for group in up_groups[1:] for d in group))
    gate_rows, up_rows, joined, mine, theirs = [], [], [], [], []
    far = []
    for g, group in enumerate(up_groups):
        if g == 0:
            gate_rows.append(fetch_rows(group, after(w_gate, chosen[0]), features))
            own[g] = after(own[g], gate_rows[g])
        if g != 1:
            up_rows.append(fetch_rows(group, after(w_up, own[g], *joined[-1:]), features))
        if g + 1 < len(up_groups):
            gate_rows.append(fetch_rows(up_groups[g + 1], after(w_gate, up_rows[-1]), features))
        value = own[g]
        for step in range(steps - 2):
            value = hop_and_join(value, step, steps)
        received = hop(value, steps - 2, steps)
        early = hop(value, steps - 1, steps)
        if g == 0:
            received = gate(after(received, up_rows[0], gate_rows[-1], early), token)
        elif g == 1:
            near_theirs = exchange(joined[0], "dp", 1)
            near = after(joined[0], own[1])
            near_sums = gate_up(
                len(up_groups[0]), near, near_theirs, gate_rows[0], up_rows[0], None, None, None, model_width
            )
            up_rows.append(fetch_rows(group, after(w_up, near_sums[2]), features))
            received = after(received, up_rows[1], early)
        far.append((early, hop(received, steps - 1, steps)))
        value = jnp.concatenate([value, received], axis=0)
        joined.append(value)
    far_sums = None
    for g, group in enumerate(up_groups):
        last = g == len(up_groups) - 1
        weights = (gate_rows[g], up_rows[g])
        late = after(far[g][1], near_sums[2] if g == 0 else far_sums[2], joined[1])
        rows = jnp.concatenate([far[g][0], late], axis=0)
        far_theirs = exchange(rows, "dp", 1)
        if g > 0:
            near_theirs = exchange(joined[g], "dp", 1)
            near = after(joined[g], rows)
            near_sums = gate_up(
                len(group), near, near_theirs, *weights, near_sums, 0 if last else None, None, model_width
            )
            rows = after(rows, near_sums[-1])
        hidden = near_sums[0] if last else None
        far_sums = gate_up(
            len(group), rows, far_theirs, *weights, far_sums, 1 if last else None, hidden, model_width
        )
    hidden = far_sums[0]

    if experts == 4 and steps == 2:
        order = DOWN_ORDER
    else:
        order = [(kind + str(d),) for d in range(experts - 1, -1, -1) for kind in ["o", "m"] + ["h"] * steps + ["f"]]
    terms = [[] for _ in range(experts)]
    hops = [0] * experts
    outputs = [None] * experts
    done = hidden
    for entry in order:
        parts = tuple((part[0], int(part[1:])) for part in entry)
        if parts[0][0] in "om":
            for (kind, d), value in zip(parts, down(parts, after(hidden, done), w_down, features)):
                done = value
                terms[d].append(exchange(done, "dp", 1) if kind == "o" else done)
            continue
        kind, d = parts[0]
        terms[d][-1] = after(terms[d][-1], done)
        if kind == "h":
            hops[d] += 1
            done = upper_rows(terms[d])
            terms[d] = lower_rows(terms[d]) + [hop(done, steps - hops[d], steps)]
        else:
            done = sum(as_f32(term) for term in terms[d]).astype(jnp.bfloat16)
            outputs[d] = done if d == 0 else exchange(done, "expert", d)

    kept, sent = combine(pick_block, pick_live, combine_weight, outputs, here)
    return assemble(kept, exchange(sent, "dp", 1))


def solution(mesh):
    in_specs = (
        P("dp", "expert"),
        P("expert", None, "dp"),
        P("expert", None, "dp"),
        P("expert", "dp", None),
        P(),
        P(),
        P(),
    )
    out_specs = P("dp", "expert")
    return jax.shard_map(
        on_device, mesh=mesh, in_specs=in_specs, out_specs=out_specs, check_vma=False
    )
```

```python
import functools

import jax
import jax.numpy as jnp
from jax import lax
from jax.experimental import pallas as pl
from jax.experimental.pallas import tpu as pltpu
from jax.sharding import PartitionSpec as P

BLOCK = 128
HALF = BLOCK // 2
MIB = 1024 * 1024
UP_GROUPS = ((0, 1), (2, 3))
DOWN_ORDER = (
    ("o3",), ("m3", "o2"), ("h3",), ("m2", "o1"), ("h2",), ("m1", "o0", "m0"), ("h3",), ("h1",), ("h2",),
    ("h0",), ("f3",), ("h1",), ("f2",), ("h0",), ("f1",), ("f0",),
)
VMEM = pl.BlockSpec(memory_space=pltpu.VMEM)
SMEM = pl.BlockSpec(memory_space=pltpu.SMEM)
ANY = pl.BlockSpec(memory_space=pl.ANY)
HBM = pl.BlockSpec(memory_space=pltpu.HBM)


def in_hbm(value):
    return pltpu.with_memory_space_constraint(value, pltpu.HBM)


def params(mib):
    return pltpu.CompilerParams(vmem_limit_bytes=mib * MIB)


def exchange(value, axis, offset):
    count = lax.axis_size(axis)
    return lax.ppermute(value, axis, [(i, i ^ offset) for i in range(count)])


def hop(value, step, steps):
    count = lax.axis_size("dp")
    turn = [i ^ (2 << (step if i % 2 == 0 else steps - 1 - step)) for i in range(count)]
    return lax.ppermute(value, "dp", list(enumerate(turn)))


def hop_and_join(value, step, steps):
    return jnp.concatenate([value, hop(value, step, steps)], axis=0)


def after(value, *others):
    return lax.optimization_barrier((value,) + others)[0]


def as_f32(value):
    return value.astype(jnp.float32)


def upper_rows(terms):
    rows = terms[0].shape[0] // 2
    return sum(as_f32(term[rows:]) for term in terms).astype(jnp.bfloat16)


def lower_rows(terms):
    return [term[: term.shape[0] // 2] for term in terms]


def plan_kernel(count, pick_block, pick_live, tokens, near, mask, blocks, picked, live, block_sem, sem):
    here = tokens.shape[0] // BLOCK
    expert = lax.axis_index("expert")
    row = lax.axis_index("dp")
    half = row % 2
    loads = []
    for b in range(here):
        rows = pl.ds(pl.multiple_of(b * BLOCK + half * HALF, HALF), HALF)
        loads.append(pltpu.make_async_copy(tokens.at[rows], blocks.at[b], block_sem.at[b]))
    loads.append(pltpu.make_async_copy(pick_block, picked, sem.at[0]))
    loads.append(pltpu.make_async_copy(pick_live, live, sem.at[1]))
    for load in loads:
        load.start()
    for load in loads:
        load.wait()
    for c in range(count):
        slot = picked[expert ^ c, row // 2]
        taken = live[expert ^ c, row // 2] == 1
        held = taken & (slot // here == half)
        value = jnp.zeros(near.shape[1:], jnp.float32)
        for b in range(here):
            keep = jnp.where(held & (slot % here == b), jnp.float32(1), jnp.float32(0))
            value = value + keep * as_f32(blocks[b])
            away = taken & (slot // here != half) & (slot % here == b)
            mask[c * here + b] = jnp.full(mask.shape[1:], jnp.where(away, jnp.float32(1), jnp.float32(0)))
        near[c] = value.astype(jnp.bfloat16)


def plan(pick_block, pick_live, tokens, count):
    here = tokens.shape[0] // BLOCK
    features = tokens.shape[1]
    return pl.pallas_call(
        functools.partial(plan_kernel, count),
        in_specs=[HBM] * 3,
        out_specs=[VMEM, VMEM],
        out_shape=[
            jax.ShapeDtypeStruct((count, HALF, features), jnp.bfloat16),
            jax.ShapeDtypeStruct((count * here, 8, 128), jnp.float32),
        ],
        scratch_shapes=[
            pltpu.VMEM((here, HALF, features), jnp.bfloat16),
            pltpu.SMEM(pick_block.shape, pick_block.dtype),
            pltpu.SMEM(pick_live.shape, pick_live.dtype),
            pltpu.SemaphoreType.DMA((here,)),
            pltpu.SemaphoreType.DMA((2,)),
        ],
        cost_estimate=pl.CostEstimate(flops=0, bytes_accessed=0, transcendentals=0),
        compiler_params=params(6),
    )(in_hbm(pick_block), in_hbm(pick_live), in_hbm(tokens))


def select_kernel(count, near, mask, other, *outs):
    here = other.shape[0] // BLOCK
    half = lax.axis_index("dp") % 2
    blocks = []
    for b in range(here):
        rows = pl.ds(pl.multiple_of(b * BLOCK + half * HALF, HALF), HALF)
        blocks.append(as_f32(other[rows, :]))
    for c in range(count):
        value = as_f32(near[c])
        for b in range(here):
            value = value + mask[c * here + b, 0:1, 0:1] * blocks[b]
        outs[c][...] = value.astype(jnp.bfloat16)


def select(near, mask, other, count):
    shape = jax.ShapeDtypeStruct((HALF, other.shape[1]), jnp.bfloat16)
    return pl.pallas_call(
        functools.partial(select_kernel, count),
        in_specs=[VMEM] * 3,
        out_specs=[VMEM] * count,
        out_shape=[shape] * count,
        compiler_params=params(6),
    )(near, mask, other)


def marker_kernel(*refs):
    refs[-1][...] = jnp.zeros_like(refs[-1])


def marker(flops, *values):
    return pl.pallas_call(
        marker_kernel,
        in_specs=[ANY] * len(values),
        out_specs=VMEM,
        out_shape=jax.ShapeDtypeStruct((8, 128), jnp.float32),
        cost_estimate=pl.CostEstimate(flops=flops, bytes_accessed=0, transcendentals=0),
        compiler_params=params(1),
    )(*values)


def gate_kernel(*refs):
    pass


def gate(value, *others):
    return pl.pallas_call(
        gate_kernel,
        in_specs=[ANY] * (1 + len(others)),
        out_specs=ANY,
        out_shape=jax.ShapeDtypeStruct(value.shape, value.dtype),
        input_output_aliases={0: 0},
        cost_estimate=pl.CostEstimate(flops=0, bytes_accessed=0, transcendentals=0),
        compiler_params=params(1),
    )(value, *others)


def row_copies(offset, place, features, weight, out, sem):
    begin = pl.multiple_of((lax.axis_index("expert") ^ offset) * features, features)
    target = out.at[pl.ds(place * features, features)]
    return [pltpu.make_async_copy(weight.at[0, pl.ds(begin, features)], target, sem)]


def fetch_kernel(group, features, weight, out, sem):
    copies = []
    for c, offset in enumerate(group):
        copies += row_copies(offset, c, features, weight, out, sem.at[c])
    for copy in copies:
        copy.start()
    for copy in copies:
        copy.wait()


def fetch_rows(group, weight, features):
    rows = len(group) * features
    hid = weight.shape[2]
    return pl.pallas_call(
        functools.partial(fetch_kernel, group, features),
        in_specs=[HBM],
        out_specs=VMEM,
        out_shape=pltpu.VMEM((rows, hid), jnp.bfloat16),
        scratch_shapes=[pltpu.SemaphoreType.DMA((len(group),))],
        cost_estimate=pl.CostEstimate(flops=0, bytes_accessed=0, transcendentals=0),
        compiler_params=params(4),
    )(in_hbm(weight))


def gate_up_kernel(count, first, place, model_width, mine, theirs, w_gate, w_up, *refs):
    last = place is not None
    if not first:
        gate_in, up_in, squares_in = refs[:3]
        refs = refs[3:]
    if last:
        hidden_out, xs, squares = refs[-3:]
    else:
        gate_out, up_out, squares, xs = refs
    features = mine.shape[1]
    half = xs.shape[0] // 2
    total = jnp.zeros((2 * half, 1), jnp.float32)
    for c in range(count):
        columns = slice(c * features, (c + 1) * features)
        for k, source in enumerate((mine, theirs)):
            for j in range(half // HALF):
                begin = (j * count + c) * HALF
                xs[k * half + j * HALF : k * half + (j + 1) * HALF, columns] = source[begin : begin + HALF, :]
        values = as_f32(xs[:, columns])
        total = total + jnp.sum(values * values, axis=1, keepdims=True)
    total = jnp.broadcast_to(total, squares.shape)
    squares[...] = total if first else total + squares_in[...]
    if last:
        inv_rms = lax.rsqrt(squares[:, :1] / model_width + 1e-05)
    hid = w_gate.shape[1]
    block = next(size for size in (256, 128) if hid % size == 0)

    for b in range(hid // block):
        cols = slice(b * block, (b + 1) * block)
        gate = None if first else gate_in[:, cols]
        up = None if first else up_in[:, cols]
        for c in range(count):
            part = xs[:, c * features : (c + 1) * features]
            rows = slice(c * features, (c + 1) * features)
            dot_gate = jnp.dot(part, w_gate[rows, cols], preferred_element_type=jnp.float32)
            dot_up = jnp.dot(part, w_up[rows, cols], preferred_element_type=jnp.float32)
            gate = dot_gate if gate is None else gate + dot_gate
            up = dot_up if up is None else up + dot_up
        if last:
            gate = gate * inv_rms
            value = (gate / (1.0 + jnp.exp(-gate)) * (up * inv_rms)).astype(jnp.bfloat16)
            hidden_out[place * half : (place + 1) * half, cols] = value[:half]
            hidden_out[(2 + place) * half : (3 + place) * half, cols] = value[half:]
        else:
            gate_out[:, cols] = gate
            up_out[:, cols] = up


def gate_up(count, mine, theirs, gate_rows, up_rows, carry, place, hidden, model_width):
    first = carry is None
    features = mine.shape[1]
    rows = 2 * mine.shape[0] // count
    hid = gate_rows.shape[1]
    acc = pltpu.VMEM((rows, hid), jnp.float32)
    scratch = [pltpu.VMEM((rows, count * features), jnp.bfloat16)]
    operands = [mine, theirs, gate_rows, up_rows] + list(carry or ())
    in_specs = [VMEM] * len(operands)
    aliases = {}
    if place is not None:
        out_shape = [pltpu.VMEM((2 * rows, hid), jnp.bfloat16)]
        scratch.append(pltpu.VMEM((rows, 128), jnp.float32))
        if hidden is not None:
            aliases = {len(operands): 0}
            operands.append(hidden)
            in_specs.append(ANY)
    else:
        out_shape = [acc, acc, pltpu.VMEM((rows, 128), jnp.float32)]
        if not first:
            aliases = {4: 0, 5: 1, 6: 2}
    return pl.pallas_call(
        functools.partial(gate_up_kernel, count, first, place, model_width),
        in_specs=in_specs,
        out_specs=[VMEM] * len(out_shape),
        out_shape=out_shape,
        scratch_shapes=scratch,
        input_output_aliases=aliases,
        cost_estimate=pl.CostEstimate(
            flops=4 * rows * features * count * hid,
            bytes_accessed=4 * features * count * hid,
            transcendentals=0,
        ),
        compiler_params=params(8),
    )(*operands)


def down_kernel(parts, hidden, weight, *outs):
    for (kind, offset), out in zip(parts, outs):
        rows, features = out.shape
        first_row = rows if kind == "o" else 0
        block = next(size for size in (512, 256, 128) if features % size == 0)
        for b in range(features // block):
            begin = pl.multiple_of((lax.axis_index("expert") ^ offset) * features + b * block, block)
            value = jnp.dot(
                hidden[first_row : first_row + rows, :],
                weight[0, :, pl.ds(begin, block)],
                preferred_element_type=jnp.float32,
            )
            out[:, b * block : (b + 1) * block] = value.astype(jnp.bfloat16)


def down(parts, hidden, w_down, features):
    rows = hidden.shape[0] // 2
    return pl.pallas_call(
        functools.partial(down_kernel, parts),
        in_specs=[VMEM, VMEM],
        out_specs=[VMEM] * len(parts),
        out_shape=[jax.ShapeDtypeStruct((rows, features), jnp.bfloat16)] * len(parts),
        cost_estimate=pl.CostEstimate(flops=0, bytes_accessed=0, transcendentals=0),
        compiler_params=params(8),
    )(hidden, w_down)


def combine_kernel(count, here, pick_block, pick_live, combine_weight, *refs):
    values = refs[:count]
    mine, other = refs[count:]
    expert = lax.axis_index("expert")
    row = lax.axis_index("dp")
    pair = row // 2
    half = row % 2
    for b in range(2 * here):
        slot = (half if b < here else 1 - half) * here + b % here
        total = None
        for c in range(count):
            taken = (pick_live[expert ^ c, pair] == 1) & (pick_block[expert ^ c, pair] == slot)
            coef = jnp.where(taken, combine_weight[expert ^ c, pair], jnp.float32(0))
            term = coef * as_f32(values[c][...])
            total = term if total is None else total + term
        target = mine if b < here else other
        target[b % here] = total.astype(jnp.bfloat16)


def combine(pick_block, pick_live, combine_weight, values, here):
    shape = jax.ShapeDtypeStruct((here,) + values[0].shape, jnp.bfloat16)
    return pl.pallas_call(
        functools.partial(combine_kernel, len(values), here),
        in_specs=[SMEM] * 3 + [VMEM] * len(values),
        out_specs=[VMEM, VMEM],
        out_shape=[shape, shape],
        compiler_params=params(6),
    )(pick_block, pick_live, combine_weight, *values)


def assemble_kernel(kept, received, out):
    half = lax.axis_index("dp") % 2
    for b in range(kept.shape[0]):
        out[pl.ds(pl.multiple_of(b * BLOCK + half * HALF, HALF), HALF), :] = kept[b]
        out[pl.ds(pl.multiple_of(b * BLOCK + (1 - half) * HALF, HALF), HALF), :] = received[b]


def assemble(kept, received):
    here, _, features = kept.shape
    return pl.pallas_call(
        assemble_kernel,
        in_specs=[VMEM, VMEM],
        out_specs=VMEM,
        out_shape=jax.ShapeDtypeStruct((here * BLOCK, features), jnp.bfloat16),
        compiler_params=params(6),
    )(kept, received)


def on_device(tokens, w_gate, w_up, w_down, pick_block, pick_live, combine_weight):
    experts = lax.axis_size("expert")
    steps = (lax.axis_size("dp") // 2).bit_length() - 1
    features = tokens.shape[1]
    model_width = features * experts
    here = tokens.shape[0] // BLOCK
    up_groups = UP_GROUPS if experts == 4 else tuple((d, d + 1) for d in range(0, experts, 2))

    near, mask = plan(pick_block, pick_live, tokens, experts)
    chosen = select(near, mask, exchange(tokens, "dp", 1), experts)
    arrived = [chosen[d] if d == 0 else exchange(chosen[d], "expert", d) for d in range(experts)]
    own = [jnp.concatenate([arrived[d] for d in group], axis=0) for group in up_groups]
    token = marker(3000000000, *(arrived[d] for group in up_groups[1:] for d in group))
    gate_rows, up_rows, joined, mine, theirs = [], [], [], [], []
    far = []
    for g, group in enumerate(up_groups):
        if g == 0:
            gate_rows.append(fetch_rows(group, after(w_gate, chosen[0]), features))
            own[g] = after(own[g], gate_rows[g])
        if g != 1:
            up_rows.append(fetch_rows(group, after(w_up, own[g], *joined[-1:]), features))
        if g + 1 < len(up_groups):
            gate_rows.append(fetch_rows(up_groups[g + 1], after(w_gate, up_rows[-1]), features))
        value = after(own[g], joined[0]) if g == 1 else own[g]
        for step in range(steps - 2):
            value = hop_and_join(value, step, steps)
        received = hop(value, steps - 2, steps)
        early = hop(value, steps - 1, steps)
        if g == 0:
            received = gate(after(received, up_rows[0], gate_rows[-1], early), token)
        elif g == 1:
            near_theirs = exchange(joined[0], "dp", 1)
            near = after(joined[0], own[1])
            near_sums = gate_up(
                len(up_groups[0]), near, near_theirs, gate_rows[0], up_rows[0], None, None, None, model_width
            )
            up_rows.append(fetch_rows(group, after(w_up, near_sums[2]), features))
            received = after(received, up_rows[1], early)
        far.append((early, hop(received, steps - 1, steps)))
        value = jnp.concatenate([value, received], axis=0)
        joined.append(value)
    far_sums = None
    for g, group in enumerate(up_groups):
        last = g == len(up_groups) - 1
        weights = (gate_rows[g], up_rows[g])
        late = after(far[g][1], near_sums[2] if g == 0 else far_sums[2], joined[1])
        rows = jnp.concatenate([far[g][0], late], axis=0)
        far_theirs = exchange(rows, "dp", 1)
        if g > 0:
            near_theirs = exchange(joined[g], "dp", 1)
            near = after(joined[g], rows)
            near_sums = gate_up(
                len(group), near, near_theirs, *weights, near_sums, 0 if last else None, None, model_width
            )
            rows = after(rows, near_sums[-1])
        hidden = near_sums[0] if last else None
        far_sums = gate_up(
            len(group), rows, far_theirs, *weights, far_sums, 1 if last else None, hidden, model_width
        )
    hidden = far_sums[0]

    if experts == 4 and steps == 2:
        order = DOWN_ORDER
    else:
        order = [(kind + str(d),) for d in range(experts - 1, -1, -1) for kind in ["o", "m"] + ["h"] * steps + ["f"]]
    terms = [[] for _ in range(experts)]
    hops = [0] * experts
    outputs = [None] * experts
    done = hidden
    for entry in order:
        parts = tuple((part[0], int(part[1:])) for part in entry)
        if parts[0][0] in "om":
            for (kind, d), value in zip(parts, down(parts, after(hidden, done), w_down, features)):
                done = value
                terms[d].append(exchange(done, "dp", 1) if kind == "o" else done)
            continue
        kind, d = parts[0]
        terms[d][-1] = after(terms[d][-1], done)
        if kind == "h":
            hops[d] += 1
            done = upper_rows(terms[d])
            terms[d] = lower_rows(terms[d]) + [hop(done, steps - hops[d], steps)]
        else:
            done = sum(as_f32(term) for term in terms[d]).astype(jnp.bfloat16)
            outputs[d] = done if d == 0 else exchange(done, "expert", d)

    kept, sent = combine(pick_block, pick_live, combine_weight, outputs, here)
    return assemble(kept, exchange(sent, "dp", 1))


def solution(mesh):
    in_specs = (
        P("dp", "expert"),
        P("expert", None, "dp"),
        P("expert", None, "dp"),
        P("expert", "dp", None),
        P(),
        P(),
        P(),
    )
    out_specs = P("dp", "expert")
    return jax.shard_map(
        on_device, mesh=mesh, in_specs=in_specs, out_specs=out_specs, check_vma=False
    )
```
